32 devices in a mesh: bond: 8 (over y, x, core), leg: 4 (over z).
Axes of the slice: x: 2, y: 2, z: 4, core: 2. Of those that a mesh axis runs over, the one named last changes fastest.
Arguments:
- amplitudes: float32 [2, 1024, 262144], P(None, 'bond', 'leg'), may hold values from -6 to 6
- vectors: float32 [64, 262144], P(None, ('leg', 'bond')), may hold values from -0.01171875 to 0.01171875
- row_map: float32 [64, 4096], P('leg'), may hold values from -0.09375 to 0.09375
- col_map: float32 [64, 4096], P('bond'), may hold values from -0.09375 to 0.09375
Outputs:
- coarse: float32 [2, 8, 64, 64], P(None, None, 'leg', 'bond')
The draws below stay inside these ranges and needn't reach their ends.
All inputs are finite; a program needn't handle non-finite values.
Results may differ from the reference program's by a relative error of at most 0.00014.
Values sent between devices are 32-bit elements; how exact they have to be, the bound alone decides.
No kernel may reach another device: no remote copies, remote signals or barrier semaphores. Data moves between devices by JAX's collectives and lax.ppermute only.
A program may use at most 128 MiB of HBM per device.

```python
import jax
import jax.numpy as jnp
from jax import lax

D = 64
K = 262144
ZS = 16


def block_levels(rng, dims, split, least, largest):
    def one(position, parts):
        steps = jax.random.uniform(jax.random.fold_in(jax.random.fold_in(rng, 6), position), (parts,), jnp.float32, least / len(split), largest / len(split))
        return jnp.repeat(jnp.exp(steps), dims[position] // parts).reshape((-1,) + (1,) * (len(dims) - position - 1))

    gain = one(*split[0])
    for cut in split[1:]:
        gain = gain * one(*cut)
    return gain


def centred(own_key, shape, deviation, limit, shards=(), held_as=jnp.bfloat16):
    level = block_levels(own_key, shape, shards, -0.22, 0.18) if shards else 1.0
    drawn = jax.random.normal(own_key, shape, jnp.float32) * deviation * level
    return jnp.minimum(jnp.maximum(drawn, -limit), limit).astype(held_as)


def setup_inputs(seed: int = 0) -> dict:
    keys = jax.random.split(jax.random.key(seed), 5)
    amplitudes = centred(keys[0], (2, ZS * D, K), 1.0, 6.0, ((1, 8), (2, 4)), jnp.float32)
    vectors = centred(keys[1], (D, K), K ** -0.5, 0.01171875, ((1, 32),), jnp.float32)
    row_map = centred(keys[2], (D, D * D), (D * D) ** -0.5, 0.09375, ((0, 4),), jnp.float32)
    col_map = centred(keys[3], (D, D * D), (D * D) ** -0.5, 0.09375, ((0, 8),), jnp.float32)
    return {"amplitudes": amplitudes, "vectors": vectors, "row_map": row_map, "col_map": col_map}


def coarsen(slab, row_maps, col_maps):
    highest = lax.Precision.HIGHEST
    even = slab[:, 0::2]
    odd = slab[:, 1::2]
    inner = jnp.einsum('ztjc,qcd->ztqjd', even, col_maps, precision=highest)
    real_part = jnp.einsum('tqjd,tkd->tqjk', inner[0], odd[0], precision=highest) - jnp.einsum('tqjd,tkd->tqjk', inner[1], odd[1], precision=highest)
    imag_part = jnp.einsum('tqjd,tkd->tqjk', inner[0], odd[1], precision=highest) + jnp.einsum('tqjd,tkd->tqjk', inner[1], odd[0], precision=highest)
    paired = jnp.stack([real_part, imag_part])
    return jnp.einsum('pjk,ztqjk->ztpq', row_maps, paired, precision=highest)


def reference(amplitudes, vectors, row_map, col_map):
    projected = jnp.einsum('jk,zrk->zjr', vectors, amplitudes, precision=lax.Precision.HIGHEST)
    slab = projected.reshape(2, D, ZS, D).transpose(0, 2, 1, 3)
    return coarsen(slab, row_map.reshape(D, D, D), col_map.reshape(D, D, D))
```

```python
import functools

import jax
import jax.numpy as jnp
import numpy as np
from jax import lax
from jax.experimental import pallas as pl
from jax.experimental.pallas import tpu as pltpu
from jax.sharding import PartitionSpec as P

LANES = 128


def split_bf16(x):
    hi = x.astype(jnp.bfloat16)
    return hi, (x - hi.astype(jnp.float32)).astype(jnp.bfloat16)


def project_kernel(spans, table, amp, *refs):
    count = len(spans)
    blocks, start, out, both = refs[:count], refs[count], refs[count + 1], refs[count + 2]
    step = pl.program_id(0)
    bond_dim = both.shape[0] // 2
    for index, (first, last) in enumerate(spans):

        @pl.when((step >= first) & (step < last))
        def _():
            hi, lo = split_bf16(blocks[index][...])
            both[:bond_dim, :] = hi
            both[bond_dim:, :] = lo

    @pl.when(step == 0)
    def _():
        out[...] = start[...]

    hi, lo = split_bf16(amp[...].reshape(-1, amp.shape[-1]))
    dims = (((1,), (1,)), ((), ()))
    out[...] += lax.dot_general(
        hi, both[...], dims, preferred_element_type=jnp.float32
    ) + lax.dot_general(lo, both[...], dims, preferred_element_type=jnp.float32)


def project(row, table, amplitudes, blocks, unit, start):
    parts, rows, _ = amplitudes.shape
    bond_dim = blocks[0].shape[0]
    spans = []
    for block in blocks:
        first = spans[-1][1] if spans else 0
        spans.append((first, first + block.shape[1] // unit))
    steps = spans[-1][1]
    whole = lambda i, t: (0, 0)

    def columns(first, last):
        return lambda i, t: (0, jnp.clip(i - first, 0, last - first - 1))

    grid_spec = pltpu.PrefetchScalarGridSpec(
        num_scalar_prefetch=1,
        grid=(steps,),
        in_specs=[pl.BlockSpec((parts, rows, unit), lambda i, t: (0, 0, t[row, i]))]
        + [pl.BlockSpec((bond_dim, unit), columns(*span)) for span in spans]
        + [pl.BlockSpec(start.shape, whole)],
        out_specs=pl.BlockSpec(start.shape, whole),
        scratch_shapes=[pltpu.VMEM((2 * bond_dim, unit), jnp.bfloat16)],
    )
    return pl.pallas_call(
        functools.partial(project_kernel, spans),
        grid_spec=grid_spec,
        out_shape=jax.ShapeDtypeStruct(start.shape, jnp.float32),
        input_output_aliases={len(blocks) + 2: 0},
        compiler_params=pltpu.CompilerParams(
            dimension_semantics=("arbitrary",), vmem_limit_bytes=20 * 2**20
        ),
        cost_estimate=pl.CostEstimate(
            flops=8 * steps * bond_dim * parts * rows * unit,
            bytes_accessed=4 * steps * unit * (parts * rows + bond_dim),
            transcendentals=0,
        ),
    )(table, amplitudes, *blocks, start)


def coarsen(slab, row_maps, col_maps):
    highest = lax.Precision.HIGHEST
    even = slab[:, 0::2]
    odd = slab[:, 1::2]
    inner = jnp.einsum("ztjc,qcd->ztqjd", even, col_maps, precision=highest)
    real_part = jnp.einsum("tqjd,tkd->tqjk", inner[0], odd[0], precision=highest) - jnp.einsum(
        "tqjd,tkd->tqjk", inner[1], odd[1], precision=highest
    )
    imag_part = jnp.einsum("tqjd,tkd->tqjk", inner[0], odd[1], precision=highest) + jnp.einsum(
        "tqjd,tkd->tqjk", inner[1], odd[0], precision=highest
    )
    paired = jnp.stack([real_part, imag_part])
    return jnp.einsum("pjk,ztqjk->ztpq", row_maps, paired, precision=highest)


def swap(x, axis, size, mask):
    return lax.ppermute(x, axis, [(i, i ^ mask) for i in range(size)])


def after(x, *others):
    return lax.optimization_barrier((x, *others))[0]


def make_rounds(dims, parts, halves):
    fresh = [[(0, p * halves + h) for h in range(halves)] for p in range(parts)]
    older = [[] for _ in range(parts)]
    rounds = []
    for step in range(dims):
        masks = [2 << ((p + step) % dims) for p in range(parts)]
        older = [fresh[p] + older[p] for p in range(parts)]
        fresh = [[(o ^ masks[p], i) for o, i in older[p]] for p in range(parts)]
        for turn in range(len(older[0])):
            rounds.append([(masks[p], older[p][turn], fresh[p][turn]) for p in range(parts)])
    return rounds


def gather_and_project(amplitudes, vectors, size):
    bond_dim, width = vectors.shape
    dims = (size // 2).bit_length() - 1
    parts = dims if dims and width % (dims * LANES) == 0 else 1
    halves = 2 if width % (2 * parts * LANES) == 0 else 1
    unit = width // (parts * halves)
    per_device = parts * halves
    rounds = make_rounds(dims, parts, halves)

    groups = [[(mask, i) for i in range(per_device)] for mask in (0, 1)]
    for turn in rounds:
        got = [block for _, _, block in turn]
        groups.append(got + [(origin ^ 1, i) for origin, i in got])
    longest = max(len(g) for g in groups)
    groups = [g + [(0, 0)] * (longest - len(g)) for g in groups]
    where = np.array(groups, np.int32)
    table = (lax.axis_index("bond") ^ where[:, :, 0]) * per_device + where[:, :, 1]

    held = {(0, i): vectors[:, i * unit : (i + 1) * unit] for i in range(per_device)}
    total = jnp.zeros((amplitudes.shape[0] * amplitudes.shape[1], 2 * bond_dim), jnp.float32)
    other = swap(vectors, "bond", size, 1)
    add = lambda row, blocks, total: project(row, table, amplitudes, blocks, unit, total)
    arrived = []
    pending = [lambda total: add(0, [vectors], total), lambda total: add(1, [other], total)]
    for number, turn in enumerate(rounds):
        got = []
        for mask, sent, block in turn:
            array = held[sent]
            if number >= 2:
                array = after(array, total, *arrived[number - 2])
            held[block] = swap(array, "bond", size, mask)
            got.append(held[block])
        arrived.append(got)
        if number >= 1:
            if number >= 2:
                total = after(total, *arrived[number - 2])
            total = pending[number - 1](total)
        twin = [swap(array, "bond", size, 1) for array in got]
        pending.append(functools.partial(add, number + 2, got + twin))
    for step in pending[max(len(rounds) - 1, 0) :]:
        total = step(total)
    return total


def local(bond, leg, amplitudes, vectors, row_map, col_map):
    bond_dim = vectors.shape[0]
    total = gather_and_project(amplitudes, vectors, bond)
    total = total[:, :bond_dim] + total[:, bond_dim:]
    mask = 1
    while mask < leg:
        total = total + swap(total, "leg", leg, mask)
        mask *= 2
    part = total.reshape(amplitudes.shape[0], amplitudes.shape[1], bond_dim).transpose(0, 2, 1)
    projected = lax.all_gather(part, "bond", axis=2, tiled=True)
    slab_count = projected.shape[2] // bond_dim
    slab = projected.reshape(2, bond_dim, slab_count, bond_dim).transpose(0, 2, 1, 3)
    row_maps = row_map.reshape(row_map.shape[0], bond_dim, bond_dim)
    col_maps = col_map.reshape(col_map.shape[0], bond_dim, bond_dim)
    return coarsen(slab, row_maps, col_maps)


def solution(mesh):
    return jax.shard_map(
        functools.partial(local, mesh.shape["bond"], mesh.shape["leg"]),
        mesh=mesh,
        in_specs=(
            P(None, "bond", "leg"),
            P(None, ("leg", "bond")),
            P("leg", None),
            P("bond", None),
        ),
        out_specs=P(None, None, "leg", "bond"),
        check_vma=False,
    )
```

```python
import functools
import math

import jax
import jax.numpy as jnp
import numpy as np
from jax import lax
from jax.experimental import pallas as pl
from jax.experimental.pallas import tpu as pltpu
from jax.sharding import PartitionSpec as P

LANES = 128
STEP = 2048
TWIN_CUTS = 2
TRANSPOSED = (((1,), (1,)), ((), ()))
PLAIN = (((1,), (0,)), ((), ()))


def split_bf16(x):
    hi = x.astype(jnp.bfloat16)
    return hi, (x - hi.astype(jnp.float32)).astype(jnp.bfloat16)


def dot(a, b, dims):
    return lax.dot_general(a, b, dims, preferred_element_type=jnp.float32)


def project_kernel(places, block_width, row, last, table, amp, *refs):
    count = 1 + max(place[0] for place in places)
    blocks, start, out = refs[:count], refs[count], refs[count + 1]
    amp_slots, block_slots, both, total, amp_sems, block_sems = refs[count + 2 :]
    steps, bond_dim, unit = block_slots.shape
    for step, (which, position, column, offset) in enumerate(places):
        here = pl.ds(pl.multiple_of(table[row, column] * block_width + offset, LANES), unit)
        pltpu.make_async_copy(amp.at[:, :, here], amp_slots.at[step], amp_sems.at[step]).start()
        there = pl.ds(position, unit)
        pltpu.make_async_copy(blocks[which].at[:, there], block_slots.at[step], block_sems.at[step]).start()
    total[...] = start[...]

    def body(step, carry):
        pltpu.make_async_copy(
            blocks[0].at[:, pl.ds(0, unit)], block_slots.at[step], block_sems.at[step]
        ).wait()
        hi, lo = split_bf16(block_slots[step])
        both[:bond_dim, :] = hi
        both[bond_dim:, :] = lo
        pltpu.make_async_copy(
            amp.at[:, :, pl.ds(0, unit)], amp_slots.at[step], amp_sems.at[step]
        ).wait()
        hi, lo = split_bf16(amp_slots[step].reshape(-1, unit))
        weights = both[...]
        total[...] += dot(hi, weights, TRANSPOSED) + dot(lo, weights, TRANSPOSED)
        return carry

    lax.fori_loop(0, steps, body, 0)
    if last:
        out[...] = (total[:, :bond_dim] + total[:, bond_dim:]).T
    else:
        out[...] = total[...]


def project(table, row, column, amplitudes, blocks, unit, start, last=False):
    step = functools.reduce(math.gcd, [block.shape[1] for block in blocks], unit)
    step = STEP if step % STEP == 0 else step
    parts, rows, _ = amplitudes.shape
    bond_dim = blocks[0].shape[0]
    places = []
    offset = column * unit
    for which, block in enumerate(blocks):
        for position in range(0, block.shape[1], step):
            places.append((which, position, offset // unit, offset % unit))
            offset += step
    steps = len(places)
    shape = (bond_dim, parts * rows) if last else start.shape
    vmem = pl.BlockSpec(memory_space=pltpu.VMEM)
    anywhere = pl.BlockSpec(memory_space=pl.ANY)
    scratch = 4 * steps * step * (parts * rows + bond_dim)
    return pl.pallas_call(
        functools.partial(project_kernel, places, unit, row, last),
        in_specs=[pl.BlockSpec(memory_space=pltpu.SMEM), anywhere] + [anywhere] * len(blocks) + [vmem],
        out_specs=vmem,
        out_shape=jax.ShapeDtypeStruct(shape, jnp.float32),
        scratch_shapes=[
            pltpu.VMEM((steps, parts, rows, step), jnp.float32),
            pltpu.VMEM((steps, bond_dim, step), jnp.float32),
            pltpu.VMEM((2 * bond_dim, step), jnp.bfloat16),
            pltpu.VMEM(start.shape, jnp.float32),
            pltpu.SemaphoreType.DMA((steps,)),
            pltpu.SemaphoreType.DMA((steps,)),
        ],
        compiler_params=pltpu.CompilerParams(vmem_limit_bytes=scratch + 10 * 2**20),
        cost_estimate=pl.CostEstimate(
            flops=8 * steps * bond_dim * parts * rows * step,
            bytes_accessed=4 * steps * step * (parts * rows + bond_dim),
            transcendentals=0,
        ),
    )(table, amplitudes, *blocks, start)


def coarsen_kernel(rows_q, slab, first_hi, first_lo, third, out, paired):
    pairs, bond_dim, lanes = slab.shape
    wide = 2 * bond_dim
    hi, lo = split_bf16(slab[...].reshape(pairs * bond_dim, lanes))
    inner = dot(hi, first_hi[...], PLAIN) + dot(lo, first_hi[...], PLAIN) + dot(hi, first_lo[...], PLAIN)
    for t in range(pairs):
        here = inner[t * bond_dim : (t + 1) * bond_dim]
        left = jnp.concatenate([here[:, q * wide : (q + 1) * wide] for q in range(rows_q)], 0)
        real = slab[t, :, bond_dim : 2 * bond_dim]
        imag = slab[t, :, 3 * bond_dim : 4 * bond_dim]
        right = jnp.concatenate(
            [jnp.concatenate([real, -imag], 1), jnp.concatenate([imag, real], 1)], 0
        )
        left_hi, left_lo = split_bf16(left)
        right_hi, right_lo = split_bf16(right)
        size = rows_q * bond_dim
        paired[t * size : (t + 1) * size, :] = (
            dot(left_hi, right_hi, TRANSPOSED)
            + dot(left_lo, right_hi, TRANSPOSED)
            + dot(left_hi, right_lo, TRANSPOSED)
        )
    count = pairs * rows_q
    total = jnp.zeros((2 * count, third.shape[0]), jnp.float32)
    for j in range(0, bond_dim, 2):
        columns = [paired[pl.ds(j + i, count, stride=bond_dim), :] for i in range(2)]
        hi, lo = split_bf16(jnp.concatenate(columns, 1))
        both = jnp.concatenate([hi, lo], 0)
        total += dot(both, third[:, j * wide : (j + 2) * wide], TRANSPOSED)
    half = third.shape[0] // 2
    result = total[:count, :half] + total[count:, :half] + total[:count, half:]
    rows_p = half // 2
    out[0] = result[:, :rows_p]
    out[1] = result[:, rows_p:]


def coarsen(slab, weights):
    first_hi, first_lo, third = weights
    pairs, bond_dim, _ = slab.shape
    rows_q = first_hi.shape[1] // (2 * bond_dim)
    rows_p = third.shape[0] // 4
    out = pl.pallas_call(
        functools.partial(coarsen_kernel, rows_q),
        in_specs=[pl.BlockSpec(memory_space=pltpu.VMEM)] * 4,
        out_specs=pl.BlockSpec(memory_space=pltpu.VMEM),
        out_shape=jax.ShapeDtypeStruct((2, pairs * rows_q, rows_p), jnp.float32),
        scratch_shapes=[pltpu.VMEM((pairs * rows_q * bond_dim, 2 * bond_dim), jnp.float32)],
        compiler_params=pltpu.CompilerParams(vmem_limit_bytes=40 * 2**20),
    )(slab, first_hi, first_lo, third)
    return out.reshape(2, pairs, rows_q, rows_p).transpose(0, 1, 3, 2)


def rounded_split(x):
    hi = lax.reduce_precision(x, exponent_bits=8, mantissa_bits=7)
    return hi.astype(jnp.bfloat16), (x - hi).astype(jnp.bfloat16)


def coarsen_weights(row_map, col_map, bond_dim):
    rows_q, rows_p = col_map.shape[0], row_map.shape[0]
    cols = col_map.reshape(rows_q, bond_dim, bond_dim).transpose(1, 0, 2)
    zero = jnp.zeros_like(cols)
    real = jnp.stack([cols, zero], 2).reshape(bond_dim, -1)
    imag = jnp.stack([zero, cols], 2).reshape(bond_dim, -1)
    gap = jnp.zeros_like(real)
    first_hi, first_lo = rounded_split(jnp.concatenate([real, gap, imag, gap], 0))
    rows = row_map.reshape(rows_p, bond_dim, bond_dim)
    zero = jnp.zeros_like(rows)
    third = jnp.concatenate([jnp.concatenate([rows, zero], 2), jnp.concatenate([zero, rows], 2)], 0)
    third = third.reshape(2 * rows_p, -1)
    return first_hi, first_lo, jnp.concatenate(rounded_split(third), 0)


def swap(x, axis, size, partner):
    return lax.ppermute(x, axis, [(i, partner(i)) for i in range(size)])


def twin(device):
    return device ^ 1


def after(x, *others):
    return lax.optimization_barrier((x, *others))[0]


def gather_and_project(amplitudes, vectors, size, weights):
    bond_dim, width = vectors.shape
    dims = (size // 2).bit_length() - 1
    halves = 2 if width % (2 * LANES) == 0 else 1
    unit = width // halves

    held = [(0, 0, h) for h in range(halves)]
    rounds = []
    for step in range(dims):
        masks = [2 << ((core + step) % dims) for core in range(2)]
        got = [(first ^ masks[0], second ^ masks[1], h) for first, second, h in held]
        rounds += [(masks, sent, block) for sent, block in zip(held, got)]
        held = held + got

    def both(blocks):
        return blocks + [(second ^ 1, first ^ 1, h) for first, second, h in blocks]

    groups = [both(held[:halves])] + [both([block]) for _, _, block in rounds]
    longest = max(len(g) for g in groups)
    where = np.array([g + [(0, 0, 0)] * (longest - len(g)) for g in groups], np.int32)
    me = lax.axis_index("bond")
    origin = me ^ jnp.where(me % 2 == 0, where[:, :, 0], where[:, :, 1])
    table = origin * halves + where[:, :, 2]

    arrays = {block: vectors[:, block[2] * unit : (block[2] + 1) * unit] for block in held[:halves]}
    total = jnp.zeros((amplitudes.shape[0] * amplitudes.shape[1], 2 * bond_dim), jnp.float32)
    add = functools.partial(project, table)
    arrived = []
    totals = [total]
    products = [lambda total: add(0, 0, amplitudes, [vectors], unit, total)]

    def products_done(count):
        while len(totals) <= count:
            totals.append(products[len(totals) - 1](totals[-1]))
        return totals[count]

    for number, (masks, sent, block) in enumerate(rounds):
        array = arrays[sent]
        if number >= 2:
            array = after(array, arrived[number - 2])
        if number == 3:
            array = after(array, *weights)
        if number >= 1:
            array = after(array, products_done(number))
        arrays[block] = swap(array, "bond", size, lambda i: i ^ masks[i % 2])
        arrived.append(arrays[block])
        if number == 0:
            other = swap(vectors, "bond", size, twin)
            products.append(lambda total: add(0, halves, amplitudes, [other], unit, total))
        mine = arrays[block]
        if number >= len(rounds) - 2:
            mine = after(mine, products_done(number + 2))
        cuts = TWIN_CUTS if unit % (TWIN_CUTS * LANES) == 0 else 1
        pair = [arrays[block]]
        for cut in range(cuts):
            some = mine[:, cut * unit // cuts : (cut + 1) * unit // cuts] if cuts > 1 else mine
            pair.append(swap(some, "bond", size, twin))
        products.append(
            lambda total, number=number, pair=pair: add(number + 1, 0, amplitudes, pair, unit, total)
        )
    total = products_done(len(rounds) + 1)
    if rounds:
        total = add(len(rounds), 0, amplitudes, pair[:1], unit, total)
        total = add(len(rounds), 1, amplitudes, pair[1:], unit, total, last=True)
    return total


def local(bond, leg, amplitudes, vectors, row_map, col_map):
    bond_dim = vectors.shape[0]
    parts, rows, _ = amplitudes.shape
    weights = coarsen_weights(row_map, col_map, bond_dim)
    total = gather_and_project(amplitudes, vectors, bond, weights)
    mask = 1
    while mask < leg:
        total = total + swap(total, "leg", leg, lambda i: i ^ mask)
        mask *= 2
    slab = lax.all_gather(total, "bond", axis=0)
    if rows != 2 * bond_dim:
        slab = slab.reshape(bond, bond_dim, parts, rows).transpose(1, 2, 0, 3)
        slab = slab.reshape(bond_dim, parts, -1, 2 * bond_dim).transpose(2, 0, 1, 3)
        slab = slab.reshape(-1, bond_dim, parts * 2 * bond_dim)
    return coarsen(slab, weights)


def solution(mesh):
    return jax.shard_map(
        functools.partial(local, mesh.shape["bond"], mesh.shape["leg"]),
        mesh=mesh,
        in_specs=(
            P(None, "bond", "leg"),
            P(None, ("leg", "bond")),
            P("leg", None),
            P("bond", None),
        ),
        out_specs=P(None, None, "leg", "bond"),
        check_vma=False,
    )
```

```python
import functools
import math

import jax
import jax.numpy as jnp
import numpy as np
from jax import lax
from jax.experimental import pallas as pl
from jax.experimental.pallas import tpu as pltpu
from jax.sharding import PartitionSpec as P

LANES = 128
FETCH_LAG = 1
LIMIT = 24
STEP = 2048
TWIN_CUTS = 2
TRANSPOSED = (((1,), (1,)), ((), ()))
PLAIN = (((1,), (0,)), ((), ()))


def split_bf16(x):
    hi = x.astype(jnp.bfloat16)
    return hi, (x - hi.astype(jnp.float32)).astype(jnp.bfloat16)


def dot(a, b, dims):
    return lax.dot_general(a, b, dims, preferred_element_type=jnp.float32)


def project_kernel(places, block_width, row, fetch, table, amp, *refs):
    count = 1 + max(place[0] for place in places)
    blocks, start, out = refs[:count], refs[count], refs[count + 1]
    refs = refs[count + 2 :]
    if fetch is not None:
        fetched, refs = refs[0], refs[1:]
    amp_slots, block_slots, both, total, amp_sems, block_sems, fetch_sem = refs
    steps, bond_dim, unit = block_slots.shape
    for step, (which, position, column, offset) in enumerate(places):
        here = pl.ds(pl.multiple_of(table[row, column] * block_width + offset, LANES), unit)
        pltpu.make_async_copy(amp.at[:, :, here], amp_slots.at[step], amp_sems.at[step]).start()
        there = pl.ds(position, unit)
        pltpu.make_async_copy(blocks[which].at[:, there], block_slots.at[step], block_sems.at[step]).start()
    if fetch is not None:
        fetches = []
        for index in range(fetched.shape[0]):
            here = pl.ds(pl.multiple_of(table[fetch, index] * block_width, LANES), block_width)
            fetches.append(pltpu.make_async_copy(amp.at[:, :, here], fetched.at[index], fetch_sem.at[index]))
            fetches[-1].start()
    total[...] = start[...]

    def body(step, carry):
        pltpu.make_async_copy(
            blocks[0].at[:, pl.ds(0, unit)], block_slots.at[step], block_sems.at[step]
        ).wait()
        hi, lo = split_bf16(block_slots[step])
        both[:bond_dim, :] = hi
        both[bond_dim:, :] = lo
        pltpu.make_async_copy(
            amp.at[:, :, pl.ds(0, unit)], amp_slots.at[step], amp_sems.at[step]
        ).wait()
        hi, lo = split_bf16(amp_slots[step].reshape(-1, unit))
        weights = both[...]
        total[...] += dot(hi, weights, TRANSPOSED) + dot(lo, weights, TRANSPOSED)
        return carry

    lax.fori_loop(0, steps, body, 0)
    out[...] = total[...]
    if fetch is not None:
        for copy in fetches:
            copy.wait()


def project(table, row, column, amplitudes, blocks, unit, start, fetch=None):
    step = functools.reduce(math.gcd, [block.shape[1] for block in blocks], unit)
    step = STEP if step % STEP == 0 else step
    parts, rows, _ = amplitudes.shape
    bond_dim = blocks[0].shape[0]
    places = []
    offset = column * unit
    for which, block in enumerate(blocks):
        for position in range(0, block.shape[1], step):
            places.append((which, position, offset // unit, offset % unit))
            offset += step
    steps = len(places)
    shapes = [jax.ShapeDtypeStruct(start.shape, jnp.float32)]
    if fetch is not None:
        shapes.append(pltpu.VMEM((2, parts, rows, unit), jnp.float32))
    vmem = pl.BlockSpec(memory_space=pltpu.VMEM)
    anywhere = pl.BlockSpec(memory_space=pl.ANY)
    scratch = 4 * steps * step * (parts * rows + bond_dim)
    result = pl.pallas_call(
        functools.partial(project_kernel, places, unit, row, fetch),
        in_specs=[pl.BlockSpec(memory_space=pltpu.SMEM), anywhere] + [anywhere] * len(blocks) + [vmem],
        out_specs=[vmem] * len(shapes),
        out_shape=shapes,
        scratch_shapes=[
            pltpu.VMEM((steps, parts, rows, step), jnp.float32),
            pltpu.VMEM((steps, bond_dim, step), jnp.float32),
            pltpu.VMEM((2 * bond_dim, step), jnp.bfloat16),
            pltpu.VMEM(start.shape, jnp.float32),
            pltpu.SemaphoreType.DMA((steps,)),
            pltpu.SemaphoreType.DMA((steps,)),
            pltpu.SemaphoreType.DMA((2,)),
        ],
        compiler_params=pltpu.CompilerParams(vmem_limit_bytes=scratch + 10 * 2**20),
        cost_estimate=pl.CostEstimate(
            flops=8 * steps * bond_dim * parts * rows * step,
            bytes_accessed=4 * steps * step * (parts * rows + bond_dim),
            transcendentals=0,
        ),
    )(table, amplitudes, *blocks, start)
    return result[0] if fetch is None else result


def fetch_kernel(row, table, amp, token, fetched, sems):
    unit = fetched.shape[-1]
    copies = []
    for index in range(fetched.shape[0]):
        here = pl.ds(pl.multiple_of(table[row, index] * unit, LANES), unit)
        copies.append(pltpu.make_async_copy(amp.at[:, :, here], fetched.at[index], sems.at[index]))
        copies[-1].start()
    for copy in copies:
        copy.wait()


def fetch_columns(table, row, amplitudes, unit, token):
    parts, rows, _ = amplitudes.shape
    return pl.pallas_call(
        functools.partial(fetch_kernel, row),
        in_specs=[pl.BlockSpec(memory_space=pltpu.SMEM)] + [pl.BlockSpec(memory_space=pl.ANY)] * 2,
        out_specs=pl.BlockSpec(memory_space=pltpu.VMEM),
        out_shape=pltpu.VMEM((2, parts, rows, unit), jnp.float32),
        scratch_shapes=[pltpu.SemaphoreType.DMA((2,))],
        compiler_params=pltpu.CompilerParams(vmem_limit_bytes=16 * 2**20),
    )(table, amplitudes, token)


def project_fetched_kernel(which, step, last, fetched, *refs):
    blocks, start, out = refs[:-2], refs[-2], refs[-1]
    bond_dim = blocks[0].shape[0]
    total = start[...]
    offset = 0
    for block in blocks:
        for position in range(0, block.shape[1], step):
            hi, lo = split_bf16(block[:, position : position + step])
            weights = jnp.concatenate([hi, lo], 0)
            amp = fetched[which, :, :, offset : offset + step]
            hi, lo = split_bf16(amp.reshape(-1, step))
            total += dot(hi, weights, TRANSPOSED) + dot(lo, weights, TRANSPOSED)
            offset += step
    if last:
        out[...] = (total[:, :bond_dim] + total[:, bond_dim:]).T
    else:
        out[...] = total


def project_fetched(fetched, which, blocks, start, last=False):
    _, parts, rows, unit = fetched.shape
    bond_dim = blocks[0].shape[0]
    step = functools.reduce(math.gcd, [block.shape[1] for block in blocks], unit)
    step = STEP if step % STEP == 0 else step
    vmem = pl.BlockSpec(memory_space=pltpu.VMEM)
    shape = (bond_dim, parts * rows) if last else start.shape
    return pl.pallas_call(
        functools.partial(project_fetched_kernel, which, step, last),
        in_specs=[vmem] * (len(blocks) + 2),
        out_specs=vmem,
        out_shape=jax.ShapeDtypeStruct(shape, jnp.float32),
        compiler_params=pltpu.CompilerParams(vmem_limit_bytes=LIMIT * 2**20),
        cost_estimate=pl.CostEstimate(
            flops=8 * unit * bond_dim * parts * rows,
            bytes_accessed=4 * unit * (parts * rows + bond_dim),
            transcendentals=0,
        ),
    )(fetched, *blocks, start)


def coarsen_kernel(rows_q, slab, first_hi, first_lo, third, out, paired):
    pairs, bond_dim, lanes = slab.shape
    wide = 2 * bond_dim
    hi, lo = split_bf16(slab[...].reshape(pairs * bond_dim, lanes))
    inner = dot(hi, first_hi[...], PLAIN) + dot(lo, first_hi[...], PLAIN) + dot(hi, first_lo[...], PLAIN)
    for t in range(pairs):
        here = inner[t * bond_dim : (t + 1) * bond_dim]
        left = jnp.concatenate([here[:, q * wide : (q + 1) * wide] for q in range(rows_q)], 0)
        real = slab[t, :, bond_dim : 2 * bond_dim]
        imag = slab[t, :, 3 * bond_dim : 4 * bond_dim]
        right = jnp.concatenate(
            [jnp.concatenate([real, -imag], 1), jnp.concatenate([imag, real], 1)], 0
        )
        left_hi, left_lo = split_bf16(left)
        right_hi, right_lo = split_bf16(right)
        size = rows_q * bond_dim
        paired[t * size : (t + 1) * size, :] = (
            dot(left_hi, right_hi, TRANSPOSED)
            + dot(left_lo, right_hi, TRANSPOSED)
            + dot(left_hi, right_lo, TRANSPOSED)
        )
    count = pairs * rows_q
    total = jnp.zeros((2 * count, third.shape[0]), jnp.float32)
    for j in range(0, bond_dim, 2):
        columns = [paired[pl.ds(j + i, count, stride=bond_dim), :] for i in range(2)]
        hi, lo = split_bf16(jnp.concatenate(columns, 1))
        both = jnp.concatenate([hi, lo], 0)
        total += dot(both, third[:, j * wide : (j + 2) * wide], TRANSPOSED)
    half = third.shape[0] // 2
    result = total[:count, :half] + total[count:, :half] + total[:count, half:]
    rows_p = half // 2
    out[0] = result[:, :rows_p]
    out[1] = result[:, rows_p:]


def coarsen(slab, weights):
    first_hi, first_lo, third = weights
    pairs, bond_dim, _ = slab.shape
    rows_q = first_hi.shape[1] // (2 * bond_dim)
    rows_p = third.shape[0] // 4
    out = pl.pallas_call(
        functools.partial(coarsen_kernel, rows_q),
        in_specs=[pl.BlockSpec(memory_space=pltpu.VMEM)] * 4,
        out_specs=pl.BlockSpec(memory_space=pltpu.VMEM),
        out_shape=jax.ShapeDtypeStruct((2, pairs * rows_q, rows_p), jnp.float32),
        scratch_shapes=[pltpu.VMEM((pairs * rows_q * bond_dim, 2 * bond_dim), jnp.float32)],
        compiler_params=pltpu.CompilerParams(vmem_limit_bytes=40 * 2**20),
    )(slab, first_hi, first_lo, third)
    return out.reshape(2, pairs, rows_q, rows_p).transpose(0, 1, 3, 2)


def rounded_split(x):
    hi = lax.reduce_precision(x, exponent_bits=8, mantissa_bits=7)
    return hi.astype(jnp.bfloat16), (x - hi).astype(jnp.bfloat16)


def coarsen_weights(row_map, col_map, bond_dim):
    rows_q, rows_p = col_map.shape[0], row_map.shape[0]
    cols = col_map.reshape(rows_q, bond_dim, bond_dim).transpose(1, 0, 2)
    zero = jnp.zeros_like(cols)
    real = jnp.stack([cols, zero], 2).reshape(bond_dim, -1)
    imag = jnp.stack([zero, cols], 2).reshape(bond_dim, -1)
    gap = jnp.zeros_like(real)
    first_hi, first_lo = rounded_split(jnp.concatenate([real, gap, imag, gap], 0))
    rows = row_map.reshape(rows_p, bond_dim, bond_dim)
    zero = jnp.zeros_like(rows)
    third = jnp.concatenate([jnp.concatenate([rows, zero], 2), jnp.concatenate([zero, rows], 2)], 0)
    third = third.reshape(2 * rows_p, -1)
    return first_hi, first_lo, jnp.concatenate(rounded_split(third), 0)


def swap(x, axis, size, partner):
    return lax.ppermute(x, axis, [(i, partner(i)) for i in range(size)])


def twin(device):
    return device ^ 1


def after(x, *others):
    return lax.optimization_barrier((x, *others))[0]


def gather_and_project(amplitudes, vectors, size, weights):
    bond_dim, width = vectors.shape
    dims = (size // 2).bit_length() - 1
    halves = 2 if width % (2 * LANES) == 0 else 1
    unit = width // halves

    held = [(0, 0, h) for h in range(halves)]
    rounds = []
    for step in range(dims):
        masks = [2 << ((core + step) % dims) for core in range(2)]
        got = [(first ^ masks[0], second ^ masks[1], h) for first, second, h in held]
        rounds += [(masks, sent, block) for sent, block in zip(held, got)]
        held = held + got

    def both(blocks):
        return blocks + [(second ^ 1, first ^ 1, h) for first, second, h in blocks]

    groups = [both(held[:halves])] + [both([block]) for _, _, block in rounds]
    longest = max(len(g) for g in groups)
    where = np.array([g + [(0, 0, 0)] * (longest - len(g)) for g in groups], np.int32)
    me = lax.axis_index("bond")
    origin = me ^ jnp.where(me % 2 == 0, where[:, :, 0], where[:, :, 1])
    table = origin * halves + where[:, :, 2]

    arrays = {block: vectors[:, block[2] * unit : (block[2] + 1) * unit] for block in held[:halves]}
    total = jnp.zeros((amplitudes.shape[0] * amplitudes.shape[1], 2 * bond_dim), jnp.float32)
    add = functools.partial(project, table)
    arrived, fetched = [], []
    totals = [after(total, *arrays.values())]
    products = [lambda total: add(0, 0, amplitudes, [vectors], unit, total)]

    def products_done(count):
        while len(totals) <= count:
            totals.append(products[len(totals) - 1](totals[-1]))
        return totals[count]

    for number, (masks, sent, block) in enumerate(rounds):
        array = arrays[sent]
        if number >= 2 and number != 3:
            array = after(array, arrived[number - 2])
        if number == 3:
            array = after(array, *weights)
        if number >= 1:
            array = after(array, products_done(number))
        arrays[block] = swap(array, "bond", size, lambda i: i ^ masks[i % 2])
        arrived.append(arrays[block])
        if number == 0:
            other = swap(vectors, "bond", size, twin)
            products.append(lambda total: add(0, halves, amplitudes, [other], unit, total))
        mine = arrays[block]
        if number >= len(rounds) - 2:
            mine = after(mine, products_done(number + 2))
        cuts = TWIN_CUTS if unit % (TWIN_CUTS * LANES) == 0 else 1
        pair = [arrays[block]]
        for cut in range(cuts):
            some = mine[:, cut * unit // cuts : (cut + 1) * unit // cuts] if cuts > 1 else mine
            pair.append(swap(some, "bond", size, twin))

        def product(total, number=number, pair=pair):
            if number == len(rounds) - 2:
                fetched.append(fetch_columns(table, len(rounds), amplitudes, unit, totals[len(rounds) - 1]))
                total = after(total, fetched[0])
            return add(number + 1, 0, amplitudes, pair, unit, total)

        products.append(product)
    total = products_done(len(rounds) + 1)
    total = project_fetched(fetched[0], 0, pair[:1], total)
    return project_fetched(fetched[0], 1, pair[1:], total, last=True)


def local(bond, leg, amplitudes, vectors, row_map, col_map):
    bond_dim = vectors.shape[0]
    parts, rows, _ = amplitudes.shape
    weights = coarsen_weights(row_map, col_map, bond_dim)
    total = gather_and_project(amplitudes, vectors, bond, weights)
    mask = 1
    while mask < leg:
        total = total + swap(total, "leg", leg, lambda i: i ^ mask)
        mask *= 2
    slab = lax.all_gather(total, "bond", axis=0)
    if rows != 2 * bond_dim:
        slab = slab.reshape(bond, bond_dim, parts, rows).transpose(1, 2, 0, 3)
        slab = slab.reshape(bond_dim, parts, -1, 2 * bond_dim).transpose(2, 0, 1, 3)
        slab = slab.reshape(-1, bond_dim, parts * 2 * bond_dim)
    return coarsen(slab, weights)


def solution(mesh):
    return jax.shard_map(
        functools.partial(local, mesh.shape["bond"], mesh.shape["leg"]),
        mesh=mesh,
        in_specs=(
            P(None, "bond", "leg"),
            P(None, ("leg", "bond")),
            P("leg", None),
            P("bond", None),
        ),
        out_specs=P(None, None, "leg", "bond"),
        check_vma=False,
    )
```

```python
import functools
import math

import jax
import jax.numpy as jnp
import numpy as np
from jax import lax
from jax.experimental import pallas as pl
from jax.experimental.pallas import tpu as pltpu
from jax.sharding import PartitionSpec as P

LANES = 128
FETCH_LAG = 2
LATE = 2
LIMIT = 24
STEP = 2048
TWIN_CUTS = 2
TRANSPOSED = (((1,), (1,)), ((), ()))
PLAIN = (((1,), (0,)), ((), ()))


def split_bf16(x):
    hi = x.astype(jnp.bfloat16)
    return hi, (x - hi.astype(jnp.float32)).astype(jnp.bfloat16)


def dot(a, b, dims):
    return lax.dot_general(a, b, dims, preferred_element_type=jnp.float32)


def project_kernel(places, block_width, row, fetch, table, amp, *refs):
    count = 1 + max(place[0] for place in places)
    blocks, start, out = refs[:count], refs[count], refs[count + 1]
    refs = refs[count + 2 :]
    if fetch is not None:
        fetched, refs = refs[0], refs[1:]
    amp_slots, block_slots, both, total, amp_sems, block_sems, fetch_sem = refs
    steps, bond_dim, unit = block_slots.shape
    for step, (which, position, column, offset) in enumerate(places):
        here = pl.ds(pl.multiple_of(table[row, column] * block_width + offset, LANES), unit)
        pltpu.make_async_copy(amp.at[:, :, here], amp_slots.at[step], amp_sems.at[step]).start()
        there = pl.ds(position, unit)
        pltpu.make_async_copy(blocks[which].at[:, there], block_slots.at[step], block_sems.at[step]).start()
    if fetch is not None:
        fetches = []
        for index in range(fetched.shape[0]):
            here = pl.ds(pl.multiple_of(table[fetch, index] * block_width, LANES), block_width)
            fetches.append(pltpu.make_async_copy(amp.at[:, :, here], fetched.at[index], fetch_sem.at[index]))
            fetches[-1].start()
    total[...] = start[...]

    def body(step, carry):
        pltpu.make_async_copy(
            blocks[0].at[:, pl.ds(0, unit)], block_slots.at[step], block_sems.at[step]
        ).wait()
        hi, lo = split_bf16(block_slots[step])
        both[:bond_dim, :] = hi
        both[bond_dim:, :] = lo
        pltpu.make_async_copy(
            amp.at[:, :, pl.ds(0, unit)], amp_slots.at[step], amp_sems.at[step]
        ).wait()
        hi, lo = split_bf16(amp_slots[step].reshape(-1, unit))
        weights = both[...]
        total[...] += dot(hi, weights, TRANSPOSED) + dot(lo, weights, TRANSPOSED)
        return carry

    lax.fori_loop(0, steps, body, 0)
    out[...] = total[...]
    if fetch is not None:
        for copy in fetches:
            copy.wait()


def project(table, row, column, amplitudes, blocks, unit, start, fetch=None):
    step = functools.reduce(math.gcd, [block.shape[1] for block in blocks], unit)
    step = STEP if step % STEP == 0 else step
    parts, rows, _ = amplitudes.shape
    bond_dim = blocks[0].shape[0]
    places = []
    offset = column * unit
    for which, block in enumerate(blocks):
        for position in range(0, block.shape[1], step):
            places.append((which, position, offset // unit, offset % unit))
            offset += step
    steps = len(places)
    shapes = [jax.ShapeDtypeStruct(start.shape, jnp.float32)]
    if fetch is not None:
        shapes.append(pltpu.VMEM((2, parts, rows, unit), jnp.float32))
    vmem = pl.BlockSpec(memory_space=pltpu.VMEM)
    anywhere = pl.BlockSpec(memory_space=pl.ANY)
    scratch = 4 * steps * step * (parts * rows + bond_dim)
    result = pl.pallas_call(
        functools.partial(project_kernel, places, unit, row, fetch),
        in_specs=[pl.BlockSpec(memory_space=pltpu.SMEM), anywhere] + [anywhere] * len(blocks) + [vmem],
        out_specs=[vmem] * len(shapes),
        out_shape=shapes,
        scratch_shapes=[
            pltpu.VMEM((steps, parts, rows, step), jnp.float32),
            pltpu.VMEM((steps, bond_dim, step), jnp.float32),
            pltpu.VMEM((2 * bond_dim, step), jnp.bfloat16),
            pltpu.VMEM(start.shape, jnp.float32),
            pltpu.SemaphoreType.DMA((steps,)),
            pltpu.SemaphoreType.DMA((steps,)),
            pltpu.SemaphoreType.DMA((2,)),
        ],
        compiler_params=pltpu.CompilerParams(vmem_limit_bytes=scratch + 10 * 2**20),
        cost_estimate=pl.CostEstimate(
            flops=8 * steps * bond_dim * parts * rows * step,
            bytes_accessed=4 * steps * step * (parts * rows + bond_dim),
            transcendentals=0,
        ),
    )(table, amplitudes, *blocks, start)
    return result[0] if fetch is None else result


def project_fetched_kernel(which, step, last, fetched, *refs):
    blocks, start, out = refs[:-2], refs[-2], refs[-1]
    bond_dim = blocks[0].shape[0]
    total = start[...]
    offset = 0
    for block in blocks:
        for position in range(0, block.shape[1], step):
            hi, lo = split_bf16(block[:, position : position + step])
            weights = jnp.concatenate([hi, lo], 0)
            amp = fetched[which, :, :, offset : offset + step]
            hi, lo = split_bf16(amp.reshape(-1, step))
            total += dot(hi, weights, TRANSPOSED) + dot(lo, weights, TRANSPOSED)
            offset += step
    if last:
        out[...] = (total[:, :bond_dim] + total[:, bond_dim:]).T
    else:
        out[...] = total


def project_fetched(fetched, which, blocks, start, last=False):
    _, parts, rows, unit = fetched.shape
    bond_dim = blocks[0].shape[0]
    step = functools.reduce(math.gcd, [block.shape[1] for block in blocks], unit)
    step = STEP if step % STEP == 0 else step
    vmem = pl.BlockSpec(memory_space=pltpu.VMEM)
    shape = (bond_dim, parts * rows) if last else start.shape
    return pl.pallas_call(
        functools.partial(project_fetched_kernel, which, step, last),
        in_specs=[vmem] * (len(blocks) + 2),
        out_specs=vmem,
        out_shape=jax.ShapeDtypeStruct(shape, jnp.float32),
        compiler_params=pltpu.CompilerParams(vmem_limit_bytes=LIMIT * 2**20),
        cost_estimate=pl.CostEstimate(
            flops=8 * unit * bond_dim * parts * rows,
            bytes_accessed=4 * unit * (parts * rows + bond_dim),
            transcendentals=0,
        ),
    )(fetched, *blocks, start)


def coarsen_kernel(rows_q, slab, first_hi, first_lo, third, out, paired):
    pairs, bond_dim, lanes = slab.shape
    wide = 2 * bond_dim
    hi, lo = split_bf16(slab[...].reshape(pairs * bond_dim, lanes))
    inner = dot(hi, first_hi[...], PLAIN) + dot(lo, first_hi[...], PLAIN) + dot(hi, first_lo[...], PLAIN)
    for t in range(pairs):
        here = inner[t * bond_dim : (t + 1) * bond_dim]
        left = jnp.concatenate([here[:, q * wide : (q + 1) * wide] for q in range(rows_q)], 0)
        real = slab[t, :, bond_dim : 2 * bond_dim]
        imag = slab[t, :, 3 * bond_dim : 4 * bond_dim]
        right = jnp.concatenate(
            [jnp.concatenate([real, -imag], 1), jnp.concatenate([imag, real], 1)], 0
        )
        left_hi, left_lo = split_bf16(left)
        right_hi, right_lo = split_bf16(right)
        size = rows_q * bond_dim
        paired[t * size : (t + 1) * size, :] = (
            dot(left_hi, right_hi, TRANSPOSED)
            + dot(left_lo, right_hi, TRANSPOSED)
            + dot(left_hi, right_lo, TRANSPOSED)
        )
    count = pairs * rows_q
    total = jnp.zeros((2 * count, third.shape[0]), jnp.float32)
    for j in range(0, bond_dim, 2):
        columns = [paired[pl.ds(j + i, count, stride=bond_dim), :] for i in range(2)]
        hi, lo = split_bf16(jnp.concatenate(columns, 1))
        both = jnp.concatenate([hi, lo], 0)
        total += dot(both, third[:, j * wide : (j + 2) * wide], TRANSPOSED)
    half = third.shape[0] // 2
    result = total[:count, :half] + total[count:, :half] + total[:count, half:]
    rows_p = half // 2
    out[0] = result[:, :rows_p]
    out[1] = result[:, rows_p:]


def coarsen(slab, weights):
    first_hi, first_lo, third = weights
    pairs, bond_dim, _ = slab.shape
    rows_q = first_hi.shape[1] // (2 * bond_dim)
    rows_p = third.shape[0] // 4
    out = pl.pallas_call(
        functools.partial(coarsen_kernel, rows_q),
        in_specs=[pl.BlockSpec(memory_space=pltpu.VMEM)] * 4,
        out_specs=pl.BlockSpec(memory_space=pltpu.VMEM),
        out_shape=jax.ShapeDtypeStruct((2, pairs * rows_q, rows_p), jnp.float32),
        scratch_shapes=[pltpu.VMEM((pairs * rows_q * bond_dim, 2 * bond_dim), jnp.float32)],
        compiler_params=pltpu.CompilerParams(vmem_limit_bytes=40 * 2**20),
    )(slab, first_hi, first_lo, third)
    return out.reshape(2, pairs, rows_q, rows_p).transpose(0, 1, 3, 2)


def rounded_split(x):
    hi = lax.reduce_precision(x, exponent_bits=8, mantissa_bits=7)
    return hi.astype(jnp.bfloat16), (x - hi).astype(jnp.bfloat16)


def coarsen_weights(row_map, col_map, bond_dim):
    rows_q, rows_p = col_map.shape[0], row_map.shape[0]
    cols = col_map.reshape(rows_q, bond_dim, bond_dim).transpose(1, 0, 2)
    zero = jnp.zeros_like(cols)
    real = jnp.stack([cols, zero], 2).reshape(bond_dim, -1)
    imag = jnp.stack([zero, cols], 2).reshape(bond_dim, -1)
    gap = jnp.zeros_like(real)
    first_hi, first_lo = rounded_split(jnp.concatenate([real, gap, imag, gap], 0))
    rows = row_map.reshape(rows_p, bond_dim, bond_dim)
    zero = jnp.zeros_like(rows)
    third = jnp.concatenate([jnp.concatenate([rows, zero], 2), jnp.concatenate([zero, rows], 2)], 0)
    third = third.reshape(2 * rows_p, -1)
    return first_hi, first_lo, jnp.concatenate(rounded_split(third), 0)


def swap(x, axis, size, partner):
    return lax.ppermute(x, axis, [(i, partner(i)) for i in range(size)])


def twin(device):
    return device ^ 1


def after(x, *others):
    return lax.optimization_barrier((x, *others))[0]


def gather_and_project(amplitudes, vectors, size, weights):
    bond_dim, width = vectors.shape
    dims = (size // 2).bit_length() - 1
    halves = 2 if width % (2 * LANES) == 0 else 1
    unit = width // halves

    held = [(0, 0, h) for h in range(halves)]
    rounds = []
    for step in range(dims):
        masks = [2 << ((core + step) % dims) for core in range(2)]
        got = [(first ^ masks[0], second ^ masks[1], h) for first, second, h in held]
        rounds += [(masks, sent, block) for sent, block in zip(held, got)]
        held = held + got

    def both(blocks):
        return blocks + [(second ^ 1, first ^ 1, h) for first, second, h in blocks]

    groups = [both(held[:halves])] + [both([block]) for _, _, block in rounds]
    longest = max(len(g) for g in groups)
    where = np.array([g + [(0, 0, 0)] * (longest - len(g)) for g in groups], np.int32)
    me = lax.axis_index("bond")
    origin = me ^ jnp.where(me % 2 == 0, where[:, :, 0], where[:, :, 1])
    table = origin * halves + where[:, :, 2]

    arrays = {block: vectors[:, block[2] * unit : (block[2] + 1) * unit] for block in held[:halves]}
    total = jnp.zeros((amplitudes.shape[0] * amplitudes.shape[1], 2 * bond_dim), jnp.float32)
    add = functools.partial(project, table)
    arrived, fetched = [], {}
    totals = [after(total, *arrays.values())]
    products = [lambda total: add(0, 0, amplitudes, [vectors], unit, total)]

    def products_done(count):
        while len(totals) <= count:
            totals.append(products[len(totals) - 1](totals[-1]))
        return totals[count]

    for number, (masks, sent, block) in enumerate(rounds):
        array = arrays[sent]
        if number >= 2 and number != 3:
            array = after(array, arrived[number - 2])
        if number == 3:
            array = after(array, *weights)
        if number >= 1:
            array = after(array, products_done(number))
        arrays[block] = swap(array, "bond", size, lambda i: i ^ masks[i % 2])
        arrived.append(arrays[block])
        if number == 0:
            other = swap(vectors, "bond", size, twin)
            products.append(lambda total: add(0, halves, amplitudes, [other], unit, total))
        mine = arrays[block]
        if number >= len(rounds) - 2:
            mine = after(mine, products_done(number + 2))
        cuts = TWIN_CUTS if number >= 0 and unit % (TWIN_CUTS * LANES) == 0 else 1
        pair = [arrays[block]]
        for cut in range(cuts):
            some = mine[:, cut * unit // cuts : (cut + 1) * unit // cuts] if cuts > 1 else mine
            pair.append(swap(some, "bond", size, twin))

        def product(total, number=number, pair=pair):
            if number in fetched:
                total = project_fetched(fetched[number], 0, pair[:1], total)
                return project_fetched(fetched[number], 1, pair[1:], total, last=number == len(rounds) - 1)
            target = number + FETCH_LAG
            if target < len(rounds) - LATE:
                return add(number + 1, 0, amplitudes, pair, unit, total)
            total, fetched[target] = add(number + 1, 0, amplitudes, pair, unit, total, fetch=target + 1)
            return total

        products.append(product)
    return products_done(len(rounds) + 2)


def local(bond, leg, amplitudes, vectors, row_map, col_map):
    bond_dim = vectors.shape[0]
    parts, rows, _ = amplitudes.shape
    weights = coarsen_weights(row_map, col_map, bond_dim)
    total = gather_and_project(amplitudes, vectors, bond, weights)
    mask = 1
    while mask < leg:
        total = total + swap(total, "leg", leg, lambda i: i ^ mask)
        mask *= 2
    slab = lax.all_gather(total, "bond", axis=0)
    if rows != 2 * bond_dim:
        slab = slab.reshape(bond, bond_dim, parts, rows).transpose(1, 2, 0, 3)
        slab = slab.reshape(bond_dim, parts, -1, 2 * bond_dim).transpose(2, 0, 1, 3)
        slab = slab.reshape(-1, bond_dim, parts * 2 * bond_dim)
    return coarsen(slab, weights)


def solution(mesh):
    return jax.shard_map(
        functools.partial(local, mesh.shape["bond"], mesh.shape["leg"]),
        mesh=mesh,
        in_specs=(
            P(None, "bond", "leg"),
            P(None, ("leg", "bond")),
            P("leg", None),
            P("bond", None),
        ),
        out_specs=P(None, None, "leg", "bond"),
        check_vma=False,
    )
```

```python
import functools
import math

import jax
import jax.numpy as jnp
import numpy as np
from jax import lax
from jax.experimental import pallas as pl
from jax.experimental.pallas import tpu as pltpu
from jax.sharding import PartitionSpec as P

LANES = 128
FETCH_LAG = 2
LATE = 2
LIMIT = 24
STEP = 2048
TWIN_CUTS = 2
TRANSPOSED = (((1,), (1,)), ((), ()))
PLAIN = (((1,), (0,)), ((), ()))


def split_bf16(x):
    hi = x.astype(jnp.bfloat16)
    return hi, (x - hi.astype(jnp.float32)).astype(jnp.bfloat16)


def dot(a, b, dims):
    return lax.dot_general(a, b, dims, preferred_element_type=jnp.float32)


def project_kernel(places, block_width, row, fetch, table, amp, *refs):
    count = 1 + max(place[0] for place in places)
    blocks, start, out = refs[:count], refs[count], refs[count + 1]
    refs = refs[count + 2 :]
    if fetch is not None:
        fetched, refs = refs[0], refs[1:]
    amp_slots, block_slots, both, total, amp_sems, block_sems, fetch_sem = refs
    steps, bond_dim, unit = block_slots.shape
    for step, (which, position, column, offset) in enumerate(places):
        here = pl.ds(pl.multiple_of(table[row, column] * block_width + offset, LANES), unit)
        pltpu.make_async_copy(amp.at[:, :, here], amp_slots.at[step], amp_sems.at[step]).start()
        there = pl.ds(position, unit)
        pltpu.make_async_copy(blocks[which].at[:, there], block_slots.at[step], block_sems.at[step]).start()
    if fetch is not None:
        fetches = []
        for index in range(fetched.shape[0]):
            here = pl.ds(pl.multiple_of(table[fetch, index] * block_width, LANES), block_width)
            fetches.append(pltpu.make_async_copy(amp.at[:, :, here], fetched.at[index], fetch_sem.at[index]))
            fetches[-1].start()
    total[...] = start[...]

    def body(step, carry):
        pltpu.make_async_copy(
            blocks[0].at[:, pl.ds(0, unit)], block_slots.at[step], block_sems.at[step]
        ).wait()
        hi, lo = split_bf16(block_slots[step])
        both[:bond_dim, :] = hi
        both[bond_dim:, :] = lo
        pltpu.make_async_copy(
            amp.at[:, :, pl.ds(0, unit)], amp_slots.at[step], amp_sems.at[step]
        ).wait()
        hi, lo = split_bf16(amp_slots[step].reshape(-1, unit))
        weights = both[...]
        total[...] += dot(hi, weights, TRANSPOSED) + dot(lo, weights, TRANSPOSED)
        return carry

    lax.fori_loop(0, steps, body, 0)
    out[...] = total[...]
    if fetch is not None:
        for copy in fetches:
            copy.wait()


def project(table, row, column, amplitudes, blocks, unit, start, fetch=None):
    step = functools.reduce(math.gcd, [block.shape[1] for block in blocks], unit)
    step = STEP if step % STEP == 0 else step
    parts, rows, _ = amplitudes.shape
    bond_dim = blocks[0].shape[0]
    places = []
    offset = column * unit
    for which, block in enumerate(blocks):
        for position in range(0, block.shape[1], step):
            places.append((which, position, offset // unit, offset % unit))
            offset += step
    steps = len(places)
    shapes = [jax.ShapeDtypeStruct(start.shape, jnp.float32)]
    if fetch is not None:
        shapes.append(pltpu.VMEM((2, parts, rows, unit), jnp.float32))
    vmem = pl.BlockSpec(memory_space=pltpu.VMEM)
    anywhere = pl.BlockSpec(memory_space=pl.ANY)
    scratch = 4 * steps * step * (parts * rows + bond_dim)
    result = pl.pallas_call(
        functools.partial(project_kernel, places, unit, row, fetch),
        in_specs=[pl.BlockSpec(memory_space=pltpu.SMEM), anywhere] + [anywhere] * len(blocks) + [vmem],
        out_specs=[vmem] * len(shapes),
        out_shape=shapes,
        scratch_shapes=[
            pltpu.VMEM((steps, parts, rows, step), jnp.float32),
            pltpu.VMEM((steps, bond_dim, step), jnp.float32),
            pltpu.VMEM((2 * bond_dim, step), jnp.bfloat16),
            pltpu.VMEM(start.shape, jnp.float32),
            pltpu.SemaphoreType.DMA((steps,)),
            pltpu.SemaphoreType.DMA((steps,)),
            pltpu.SemaphoreType.DMA((2,)),
        ],
        compiler_params=pltpu.CompilerParams(vmem_limit_bytes=scratch + 10 * 2**20),
        cost_estimate=pl.CostEstimate(
            flops=8 * steps * bond_dim * parts * rows * step,
            bytes_accessed=4 * steps * step * (parts * rows + bond_dim),
            transcendentals=0,
        ),
    )(table, amplitudes, *blocks, start)
    return result[0] if fetch is None else result


def project_fetched_kernel(which, step, last, fetched, *refs):
    blocks, start, out = refs[:-2], refs[-2], refs[-1]
    bond_dim = blocks[0].shape[0]
    total = start[...]
    offset = 0
    for block in blocks:
        for position in range(0, block.shape[1], step):
            hi, lo = split_bf16(block[:, position : position + step])
            weights = jnp.concatenate([hi, lo], 0)
            amp = fetched[which, :, :, offset : offset + step]
            hi, lo = split_bf16(amp.reshape(-1, step))
            total += dot(hi, weights, TRANSPOSED) + dot(lo, weights, TRANSPOSED)
            offset += step
    if last:
        out[...] = (total[:, :bond_dim] + total[:, bond_dim:]).T
    else:
        out[...] = total


def project_fetched(fetched, which, blocks, start, last=False):
    _, parts, rows, unit = fetched.shape
    bond_dim = blocks[0].shape[0]
    step = functools.reduce(math.gcd, [block.shape[1] for block in blocks], unit)
    step = STEP if step % STEP == 0 else step
    vmem = pl.BlockSpec(memory_space=pltpu.VMEM)
    shape = (bond_dim, parts * rows) if last else start.shape
    return pl.pallas_call(
        functools.partial(project_fetched_kernel, which, step, last),
        in_specs=[vmem] * (len(blocks) + 2),
        out_specs=vmem,
        out_shape=jax.ShapeDtypeStruct(shape, jnp.float32),
        compiler_params=pltpu.CompilerParams(vmem_limit_bytes=LIMIT * 2**20),
        cost_estimate=pl.CostEstimate(
            flops=8 * unit * bond_dim * parts * rows,
            bytes_accessed=4 * unit * (parts * rows + bond_dim),
            transcendentals=0,
        ),
    )(fetched, *blocks, start)


def coarsen_kernel(rows_q, slab, first_hi, first_lo, third, out, paired):
    pairs, bond_dim, lanes = slab.shape
    wide = 2 * bond_dim
    hi, lo = split_bf16(slab[...].reshape(pairs * bond_dim, lanes))
    inner = dot(hi, first_hi[...], PLAIN) + dot(lo, first_hi[...], PLAIN) + dot(hi, first_lo[...], PLAIN)
    for t in range(pairs):
        here = inner[t * bond_dim : (t + 1) * bond_dim]
        left = jnp.concatenate([here[:, q * wide : (q + 1) * wide] for q in range(rows_q)], 0)
        real = slab[t, :, bond_dim : 2 * bond_dim]
        imag = slab[t, :, 3 * bond_dim : 4 * bond_dim]
        right = jnp.concatenate(
            [jnp.concatenate([real, -imag], 1), jnp.concatenate([imag, real], 1)], 0
        )
        left_hi, left_lo = split_bf16(left)
        right_hi, right_lo = split_bf16(right)
        size = rows_q * bond_dim
        paired[t * size : (t + 1) * size, :] = (
            dot(left_hi, right_hi, TRANSPOSED)
            + dot(left_lo, right_hi, TRANSPOSED)
            + dot(left_hi, right_lo, TRANSPOSED)
        )
    count = pairs * rows_q
    total = jnp.zeros((2 * count, third.shape[0]), jnp.float32)
    for j in range(0, bond_dim, 2):
        columns = [paired[pl.ds(j + i, count, stride=bond_dim), :] for i in range(2)]
        hi, lo = split_bf16(jnp.concatenate(columns, 1))
        both = jnp.concatenate([hi, lo], 0)
        total += dot(both, third[:, j * wide : (j + 2) * wide], TRANSPOSED)
    half = third.shape[0] // 2
    result = total[:count, :half] + total[count:, :half] + total[:count, half:]
    rows_p = half // 2
    out[0] = result[:, :rows_p]
    out[1] = result[:, rows_p:]


def coarsen(slab, weights):
    first_hi, first_lo, third = weights
    pairs, bond_dim, _ = slab.shape
    rows_q = first_hi.shape[1] // (2 * bond_dim)
    rows_p = third.shape[0] // 4
    out = pl.pallas_call(
        functools.partial(coarsen_kernel, rows_q),
        in_specs=[pl.BlockSpec(memory_space=pltpu.VMEM)] * 4,
        out_specs=pl.BlockSpec(memory_space=pltpu.VMEM),
        out_shape=jax.ShapeDtypeStruct((2, pairs * rows_q, rows_p), jnp.float32),
        scratch_shapes=[pltpu.VMEM((pairs * rows_q * bond_dim, 2 * bond_dim), jnp.float32)],
        compiler_params=pltpu.CompilerParams(vmem_limit_bytes=40 * 2**20),
    )(slab, first_hi, first_lo, third)
    return out.reshape(2, pairs, rows_q, rows_p).transpose(0, 1, 3, 2)


def rounded_split(x):
    hi = lax.reduce_precision(x, exponent_bits=8, mantissa_bits=7)
    return hi.astype(jnp.bfloat16), (x - hi).astype(jnp.bfloat16)


def coarsen_weights(row_map, col_map, bond_dim):
    rows_q, rows_p = col_map.shape[0], row_map.shape[0]
    cols = col_map.reshape(rows_q, bond_dim, bond_dim).transpose(1, 0, 2)
    zero = jnp.zeros_like(cols)
    real = jnp.stack([cols, zero], 2).reshape(bond_dim, -1)
    imag = jnp.stack([zero, cols], 2).reshape(bond_dim, -1)
    gap = jnp.zeros_like(real)
    first_hi, first_lo = rounded_split(jnp.concatenate([real, gap, imag, gap], 0))
    rows = row_map.reshape(rows_p, bond_dim, bond_dim)
    zero = jnp.zeros_like(rows)
    third = jnp.concatenate([jnp.concatenate([rows, zero], 2), jnp.concatenate([zero, rows], 2)], 0)
    third = third.reshape(2 * rows_p, -1)
    return first_hi, first_lo, jnp.concatenate(rounded_split(third), 0)


def swap(x, axis, size, partner):
    return lax.ppermute(x, axis, [(i, partner(i)) for i in range(size)])


def twin(device):
    return device ^ 1


def after(x, *others):
    return lax.optimization_barrier((x, *others))[0]


def gather_and_project(amplitudes, vectors, size, weights):
    bond_dim, width = vectors.shape
    dims = (size // 2).bit_length() - 1
    halves = 2 if width % (2 * LANES) == 0 else 1
    unit = width // halves

    held = [(0, 0, h) for h in range(halves)]
    rounds = []
    for step in range(dims):
        masks = [2 << ((core + step) % dims) for core in range(2)]
        got = [(first ^ masks[0], second ^ masks[1], h) for first, second, h in held]
        rounds += [(masks, sent, block) for sent, block in zip(held, got)]
        held = held + got

    def both(blocks):
        return blocks + [(second ^ 1, first ^ 1, h) for first, second, h in blocks]

    groups = [both(held[:halves])] + [both([block]) for _, _, block in rounds]
    longest = max(len(g) for g in groups)
    where = np.array([g + [(0, 0, 0)] * (longest - len(g)) for g in groups], np.int32)
    me = lax.axis_index("bond")
    origin = me ^ jnp.where(me % 2 == 0, where[:, :, 0], where[:, :, 1])
    table = origin * halves + where[:, :, 2]

    arrays, rest = {}, vectors
    for block in held[:halves]:
        arrays[block] = rest[:, block[2] * unit : (block[2] + 1) * unit]
        rest = after(vectors, *arrays.values())
    total = jnp.zeros((amplitudes.shape[0] * amplitudes.shape[1], 2 * bond_dim), jnp.float32)
    add = functools.partial(project, table)
    arrived, fetched = [], {}
    totals = [after(total, *arrays.values())]
    products = [lambda total: add(0, 0, amplitudes, [vectors], unit, total)]

    def products_done(count):
        while len(totals) <= count:
            totals.append(products[len(totals) - 1](totals[-1]))
        return totals[count]

    for number, (masks, sent, block) in enumerate(rounds):
        array = arrays[sent]
        if number >= 2 and number != 3:
            array = after(array, arrived[number - 2])
        if number == 3:
            array = after(array, *weights)
        if number >= 1:
            array = after(array, products_done(number))
        arrays[block] = swap(array, "bond", size, lambda i: i ^ masks[i % 2])
        arrived.append(arrays[block])
        if number == 0:
            other = swap(vectors, "bond", size, twin)
            products.append(lambda total: add(0, halves, amplitudes, [other], unit, total))
        mine = arrays[block]
        if number >= len(rounds) - 2:
            mine = after(mine, products_done(number + 2))
        cuts = TWIN_CUTS if number >= 0 and unit % (TWIN_CUTS * LANES) == 0 else 1
        pair = [arrays[block]]
        for cut in range(cuts):
            some = mine[:, cut * unit // cuts : (cut + 1) * unit // cuts] if cuts > 1 else mine
            pair.append(swap(some, "bond", size, twin))

        def product(total, number=number, pair=pair):
            if number in fetched:
                total = project_fetched(fetched[number], 0, pair[:1], total)
                return project_fetched(fetched[number], 1, pair[1:], total, last=number == len(rounds) - 1)
            target = number + FETCH_LAG
            if target < len(rounds) - LATE:
                return add(number + 1, 0, amplitudes, pair, unit, total)
            total, fetched[target] = add(number + 1, 0, amplitudes, pair, unit, total, fetch=target + 1)
            return total

        products.append(product)
    return products_done(len(rounds) + 2)


def local(bond, leg, amplitudes, vectors, row_map, col_map):
    bond_dim = vectors.shape[0]
    parts, rows, _ = amplitudes.shape
    weights = coarsen_weights(row_map, col_map, bond_dim)
    total = gather_and_project(amplitudes, vectors, bond, weights)
    mask = 1
    while mask < leg:
        total = total + swap(total, "leg", leg, lambda i: i ^ mask)
        mask *= 2
    slab = lax.all_gather(total, "bond", axis=0)
    if rows != 2 * bond_dim:
        slab = slab.reshape(bond, bond_dim, parts, rows).transpose(1, 2, 0, 3)
        slab = slab.reshape(bond_dim, parts, -1, 2 * bond_dim).transpose(2, 0, 1, 3)
        slab = slab.reshape(-1, bond_dim, parts * 2 * bond_dim)
    return coarsen(slab, weights)


def solution(mesh):
    return jax.shard_map(
        functools.partial(local, mesh.shape["bond"], mesh.shape["leg"]),
        mesh=mesh,
        in_specs=(
            P(None, "bond", "leg"),
            P(None, ("leg", "bond")),
            P("leg", None),
            P("bond", None),
        ),
        out_specs=P(None, None, "leg", "bond"),
        check_vma=False,
    )
```
